256 devices in a mesh: prow: 8 (over x, y_hi), pcol: 32 (over y_lo, z, core).
Axes of the slice: x: 4, y: 4 (y_hi: 2, y_lo: 2; y = y_hi * 2 + y_lo), z: 8, core: 2. Of those that a mesh axis runs over, the one named last changes fastest.
Arguments:
- anc_inverse: float32 [8192, 8192], P('pcol', 'prow'), may hold values from -8 to 8
- lpanel: float32 [8192, 2, 2048], P('prow', None, 'pcol'), may hold values from -6 to 6
- pattern: int32 [2, 16], replicated, may hold values from 0 to 31, as said below
Outputs:
- selected: float32 [8192, 2, 2048], P('pcol', None, 'prow')
The draws below stay inside these ranges and needn't reach their ends.
Inputs may be any that keep to these rules, and one draw needn't show every extreme that they name: `pattern`: entry q of each row is block 2q or block 2q + 1, so each row names one block of every aligned pair of blocks, in rising order, always the first and the last block.
All inputs are finite; a program needn't handle non-finite values.
Results may differ from the reference program's by a relative error of at most 0.00007.
Values sent between devices are 32-bit elements; how exact they have to be, the bound alone decides.
No kernel may reach another device: no remote copies, remote signals or barrier semaphores. Data moves between devices by JAX's collectives and lax.ppermute only.
A program may use at most 64 MiB of HBM per device.

```python
import math
import jax
import jax.numpy as jnp
from jax import lax

B = 256
NA = 8192
W = 2048
NK = 2


def draw_anc_inverse(key, part):
    key = jax.random.fold_in(key, 11)
    first_key = jax.random.fold_in(key, 0)
    raw = jax.random.truncated_normal(first_key, -4.0, 4.0, (NA, NA), jnp.float32)
    scales = jnp.ones((NA,), jnp.float32)
    symmetric = (raw + raw.T) * 0.5 ** 0.5 / math.sqrt(NA)
    symmetric = symmetric * jnp.sqrt(scales[:, None] * scales[None, :])
    ident = (lax.broadcasted_iota(jnp.int32, (NA, NA), 0) == lax.broadcasted_iota(jnp.int32, (NA, NA), 1)).astype(jnp.float32)
    return 2.0 * symmetric + ident


def draw_pattern(key, part):
    key = jax.random.fold_in(key, 5)
    pairs = NA // (2 * B)
    picks = jax.random.randint(key, (NK, pairs), 0, 2).astype(jnp.int32)
    picks = picks.at[:, 0].set(0)
    picks = picks.at[:, pairs - 1].set(1)
    return (2 * jnp.arange(pairs, dtype=jnp.int32)[None, :] + picks).astype(jnp.int32)


def block_levels(rng, dims, cuts, smallest, top_value):
    loudness, own = 1.0, jax.random.fold_in(rng, 6)
    for axis_at, shards_of in cuts:
        heights = jnp.exp(jax.random.uniform(jax.random.fold_in(own, axis_at), (shards_of,), jnp.float32, smallest / len(cuts), top_value / len(cuts)))
        loudness = loudness * jnp.repeat(heights, dims[axis_at] // shards_of).reshape([-1 if axis == axis_at else 1 for axis in range(len(dims))])
    return loudness


def scatter_about(stream_key, extent, deviation, bound, cuts=(), kind=jnp.bfloat16):
    result = deviation * jax.random.normal(stream_key, extent, jnp.float32)
    if cuts:
        result = result * block_levels(stream_key, extent, cuts, -0.22, 0.18)
    return jnp.clip(result, -bound, bound).astype(kind)


def setup_inputs(seed: int = 0) -> dict:
    key_of = jax.random.split(jax.random.key(seed), 4)
    anc_inverse = draw_anc_inverse(jax.random.fold_in(key_of[3], 71), 0)
    lpanel = scatter_about(key_of[1], (NA, NK, W), 1.0, 6.0, ((0, 8), (2, 32)), jnp.float32)
    pattern = draw_pattern(jax.random.fold_in(key_of[3], 71), 0)
    return {"anc_inverse": anc_inverse, "lpanel": lpanel, "pattern": pattern}


def reference(anc_inverse, lpanel, pattern):
    block_ids = jnp.arange(NA, dtype=jnp.int32) // B
    member = jnp.any(block_ids[:, None, None] == pattern[None, :, :], axis=2).astype(jnp.float32)
    used = lpanel * member[:, :, None]
    product = jnp.einsum("rc,ckw->rkw", anc_inverse, used, precision=lax.Precision.HIGHEST)
    return -(product * member[:, :, None])
```

```python
import jax
import jax.numpy as jnp
from jax import lax
from jax.experimental import pallas as pl
from jax.experimental.pallas import tpu as pltpu
from jax.sharding import PartitionSpec as P

B = 256
H = 128
F32 = jnp.float32
BF16 = jnp.bfloat16
AXES = ("prow", "pcol")
VMEM_LIMIT = 40 * 1024 * 1024

DEVICES = [(x, y, z, c) for x in range(4) for y in range(4) for z in range(8) for c in range(2)]


def number(x, y, z, c):
    return (2 * x + y // 2) * 32 + 16 * (y % 2) + 2 * z + c


def send(array, move):
    pairs = [(number(*d), number(*move(*d))) for d in DEVICES]
    return lax.ppermute(array, AXES, pairs)


def other_core(x, y, z, c):
    return x, y, z, 1 - c


def other_low(x, y, z, c):
    return x, y ^ 1, z, c


def other_high(x, y, z, c):
    return x, y ^ 2, z, c


def other_both(x, y, z, c):
    return x, y ^ 3, z, c


def ring(x, y, z, c):
    return x, y, (z + 1 - 2 * c) % 8, c


def along_x(step):
    return lambda x, y, z, c: ((x + step) % 4, y, z, c)


def home(x, y, z, c):
    child, low = y // 2, y % 2
    return 2 * low + x // 2, 2 * (x % 2) + c, z, child


def position():
    prow, pcol = lax.axis_index("prow"), lax.axis_index("pcol")
    return prow % 2, pcol // 16, (pcol // 2) % 8, pcol % 2, prow, pcol


def call(kernel, shapes, *args, flops=0):
    in_specs = [
        pl.BlockSpec(memory_space=pltpu.SMEM if a.dtype == jnp.int32 else pltpu.VMEM) for a in args
    ]
    shapes = [jax.ShapeDtypeStruct(s, d) for s, d in shapes]
    size = sum(a.size * a.dtype.itemsize for a in (*args, *shapes))
    return pl.pallas_call(
        kernel,
        out_shape=shapes,
        in_specs=in_specs,
        out_specs=[pl.BlockSpec(memory_space=pltpu.VMEM) for _ in shapes],
        compiler_params=pltpu.CompilerParams(vmem_limit_bytes=VMEM_LIMIT),
        cost_estimate=pl.CostEstimate(flops=flops, bytes_accessed=size, transcendentals=0),
    )(*args)


def column(pattern_ref, child, prow, t):
    block = pattern_ref[child, 2 * prow + t] - 4 * prow
    return pl.multiple_of(block * B, B)


def compact_panel(pattern_ref, panel_ref, mine_ref, other_ref):
    child, _, _, _, prow, _ = position()
    for out_ref, which in ((mine_ref, child), (other_ref, 1 - child)):
        for t in range(2):
            start = column(pattern_ref, which, prow, t)
            out_ref[:, t * B:(t + 1) * B] = panel_ref[which, :, pl.ds(start, B)]


def compact_inverse(pattern_ref, inverse_ref, keep_ref, give_ref):
    _, _, _, core, prow, _ = position()
    for out_ref, half in ((keep_ref, core), (give_ref, 1 - core)):
        rows = pl.ds(pl.multiple_of(half * H, H), H)
        for child in range(2):
            for t in range(2):
                start = column(pattern_ref, child, prow, t)
                out_ref[child, :, t * B:(t + 1) * B] = inverse_ref[rows, pl.ds(start, B)]


def choose_rows(pattern_ref, own_ref, got_ref, mine_ref, other_ref):
    child, _, _, core, _, pcol = position()
    pair = pcol // 2
    for out_ref, which in ((mine_ref, child), (other_ref, 1 - child)):
        here = pattern_ref[which, pair] - 2 * pair == core

        @pl.when(here)
        def _():
            out_ref[...] = own_ref[which]

        @pl.when(jnp.logical_not(here))
        def _():
            out_ref[...] = got_ref[which]


def split(value):
    high = value.astype(BF16)
    return high, (value - high.astype(F32)).astype(BF16)


def split_inverse(*refs):
    own, got, (high_ref, low_ref) = refs[:4], refs[4:8], refs[8:]
    _, low_y, _, core, _, _ = position()
    for half_refs, half in ((own, core), (got, 1 - core)):
        rows = pl.ds(pl.multiple_of(half * H, H), H)
        for i, ref in enumerate(half_refs):
            side = (low_y + core + i // 2) % 2
            high, low = split(ref[...])
            columns = slice((i % 2) * 2 * B, (i % 2 + 1) * 2 * B)
            high_ref[side, rows, columns] = high
            low_ref[side, rows, columns] = low


def dot(a, b):
    return lax.dot_general(a, b, (((1,), (1,)), ((), ())), preferred_element_type=F32)


def multiply(counts, *refs):
    n = len(counts)
    pieces, (high_ref, low_ref, keep_ref, give_ref) = refs[:2 * n], refs[2 * n:]
    slot = 0
    for i, count in enumerate(counts):
        parts = [split(ref[:64 * count]) for ref in pieces[2 * i:2 * i + 2]]
        for side, out_ref in enumerate((keep_ref, give_ref)):
            total = None
            for j, (high, low) in enumerate(parts):
                columns = slice(j * 2 * B, (j + 1) * 2 * B)
                a_high, a_low = high_ref[side, :, columns], low_ref[side, :, columns]
                term = dot(high, a_high) + (dot(high, a_low) + dot(low, a_high))
                total = term if total is None else total + term
            out_ref[slot:slot + count] = total.reshape(count, 64, B)
        slot += count


def product(counts, pieces, a_high, a_low):
    rows = sum(counts)
    shape = ((rows, 64, B), F32)
    return call(
        lambda *refs: multiply(counts, *refs),
        [shape, shape],
        *pieces,
        a_high,
        a_low,
        flops=2 * rows * 64 * 2 * B * 4 * B * 3,
    )


def arrange(own_early, own_late, got_early, got_late, *outs):
    _, _, z, core, prow, _ = position()
    x = prow // 2
    early = own_early.shape[0]
    for m, out_ref in enumerate(outs):
        for odd in range(2):
            z_from = 2 * ((x + m) % 4) + odd
            ahead = (z - z_from + 8) % 8
            for w_core in range(2):
                near = jnp.logical_or(ahead == 0, ahead == 4)
                source = jnp.where(near, w_core, jnp.where(ahead < 4, 0, 1))
                steps = jnp.where(ahead <= 4, ahead, 8 - ahead)
                inner = 2 * steps - 1 + jnp.where(source == w_core, 0, 1)
                slot = jnp.where(ahead == 0, 0, inner)
                here = source == core
                first = slot < early
                for ref, mine, start in (
                    (own_early, True, 0), (own_late, True, early), (got_early, False, 0), (got_late, False, early),
                ):
                    wanted = jnp.logical_and(here == mine, first == (start == 0))

                    @pl.when(wanted)
                    def _():
                        out_ref[2 * odd + w_core] = ref[slot - start]


def per_device(anc_inverse, lpanel, pattern):
    panel = jnp.transpose(lpanel, (1, 2, 0))
    half_piece = ((64, 2 * B), F32)
    mine, other = call(compact_panel, [half_piece, half_piece], pattern, panel)
    swapped = send(other, other_high)
    mine = jnp.concatenate([mine, send(mine, other_core)], axis=0)
    chain_a = [mine]

    pair = ((2, H, 2 * B), F32)
    keep, give = call(compact_inverse, [pair, pair], pattern, anc_inverse)
    got = send(give, other_core)
    quarter = ((H, 2 * B), F32)
    a_mine, a_other = call(choose_rows, [quarter, quarter], pattern, keep, got)

    chain_b = [jnp.concatenate([swapped, send(swapped, other_core)], axis=0)]
    for step in range(3):
        chain_a.append(send(chain_a[-1], ring))
        chain_b.append(send(chain_b[-1], ring))
    chain_a.append(send(chain_a[-1][:64], ring))
    chain_b.append(send(chain_b[-1][:64], ring))

    blocks = [a_mine, send(a_other, other_high), send(a_mine, other_low), send(a_other, other_both)]
    halves = [send(block, other_core) for block in blocks]
    whole = ((2, B, 4 * B), BF16)
    a_high, a_low = call(split_inverse, [whole, whole], *blocks, *halves)

    chunks = [piece for both in zip(chain_a, chain_b) for piece in both]
    keep_early, give_early = product((1, 2, 2), chunks[:6], a_high, a_low)
    keep_late, give_late = product((2, 1), chunks[6:], a_high, a_low)
    got_early = send(give_early, other_core)
    got_late = send(give_late, other_core)
    terms = call(arrange, [((4, 64, B), F32)] * 4, keep_early, keep_late, got_early, got_late)
    total = terms[0]
    for m in range(1, 4):
        total = total + send(terms[m], along_x(m))
    result = send(total, home).reshape(B, B)
    second = send(result, other_core)

    _, _, _, core, _, pcol = position()
    block = pcol
    members = jnp.any(pattern == block, axis=1)
    both = jnp.where(core == 0, jnp.stack([result, second]), jnp.stack([second, result]))
    both = jnp.where(members[:, None, None], -both, 0.0)
    return jnp.transpose(both, (2, 0, 1))


def solution(mesh):
    return jax.shard_map(
        per_device,
        mesh=mesh,
        in_specs=(P("pcol", "prow"), P("prow", None, "pcol"), P()),
        out_specs=P("pcol", None, "prow"),
        check_vma=False,
    )
```

```python
import jax
import jax.numpy as jnp
from jax import lax
from jax.experimental import pallas as pl
from jax.experimental.pallas import tpu as pltpu
from jax.sharding import PartitionSpec as P

B = 256
H = 128
F32 = jnp.float32
BF16 = jnp.bfloat16
AXES = ("prow", "pcol")
VMEM_LIMIT = 40 * 1024 * 1024

DEVICES = [(x, y, z, c) for x in range(4) for y in range(4) for z in range(8) for c in range(2)]


def number(x, y, z, c):
    return (2 * x + y // 2) * 32 + 16 * (y % 2) + 2 * z + c


def send(array, move):
    pairs = [(number(*d), number(*move(*d))) for d in DEVICES]
    return lax.ppermute(array, AXES, pairs)


def other_core(x, y, z, c):
    return x, y, z, 1 - c


def other_low(x, y, z, c):
    return x, y ^ 1, z, c


def other_high(x, y, z, c):
    return x, y ^ 2, z, c


def other_both(x, y, z, c):
    return x, y ^ 3, z, c


def ring(x, y, z, c):
    return x, y, (z + 1 - 2 * c) % 8, c


def along_x(step):
    return lambda x, y, z, c: ((x + step) % 4, y, z, c)


def spread(flip):
    return lambda x, y, z, c: (x, 2 * (y // 2 ^ flip) + c, z, y % 2)


def position():
    prow, pcol = lax.axis_index("prow"), lax.axis_index("pcol")
    return prow % 2, pcol // 16, (pcol // 2) % 8, pcol % 2, prow, pcol


def call(kernel, shapes, *args, flops=0):
    in_specs = [
        pl.BlockSpec(memory_space=pltpu.SMEM if a.dtype == jnp.int32 else pltpu.VMEM) for a in args
    ]
    shapes = [jax.ShapeDtypeStruct(s, d) for s, d in shapes]
    size = sum(a.size * a.dtype.itemsize for a in (*args, *shapes))
    return pl.pallas_call(
        kernel,
        out_shape=shapes,
        in_specs=in_specs,
        out_specs=[pl.BlockSpec(memory_space=pltpu.VMEM) for _ in shapes],
        compiler_params=pltpu.CompilerParams(vmem_limit_bytes=VMEM_LIMIT),
        cost_estimate=pl.CostEstimate(flops=flops, bytes_accessed=size, transcendentals=0),
    )(*args)


def column(pattern_ref, child, prow, t):
    block = pattern_ref[child, 2 * prow + t] - 4 * prow
    return pl.multiple_of(block * B, B)


def compact_panel(pattern_ref, panel_ref, mine_ref, other_ref):
    child, _, _, _, prow, _ = position()
    for out_ref, which in ((mine_ref, child), (other_ref, 1 - child)):
        for t in range(2):
            start = column(pattern_ref, which, prow, t)
            out_ref[:, t * B:(t + 1) * B] = panel_ref[which, :, pl.ds(start, B)]


def compact_inverse(pattern_ref, inverse_ref, keep_ref, give_ref):
    _, _, _, core, prow, _ = position()
    for out_ref, half in ((keep_ref, core), (give_ref, 1 - core)):
        rows = pl.ds(pl.multiple_of(half * H, H), H)
        for child in range(2):
            for t in range(2):
                start = column(pattern_ref, child, prow, t)
                out_ref[child, :, t * B:(t + 1) * B] = inverse_ref[rows, pl.ds(start, B)]


def choose_rows(pattern_ref, own_ref, got_ref, mine_ref, other_ref):
    child, _, _, core, _, pcol = position()
    pair = pcol // 2
    for out_ref, which in ((mine_ref, child), (other_ref, 1 - child)):
        here = pattern_ref[which, pair] - 2 * pair == core

        @pl.when(here)
        def _():
            out_ref[...] = own_ref[which]

        @pl.when(jnp.logical_not(here))
        def _():
            out_ref[...] = got_ref[which]


def split(value):
    high = value.astype(BF16)
    return high, (value - high.astype(F32)).astype(BF16)


def split_inverse(*refs):
    own, got, (high_ref, low_ref) = refs[:4], refs[4:8], refs[8:]
    _, low_y, _, core, _, _ = position()
    for half_refs, half in ((own, core), (got, 1 - core)):
        for i, ref in enumerate(half_refs):
            side = (low_y + core + i // 2) % 2
            high, low = split(ref[...].T)
            rows = slice((i % 2) * 2 * B, (i % 2 + 1) * 2 * B)
            columns = pl.ds(pl.multiple_of(side * B + half * H, H), H)
            high_ref[rows, columns] = high
            low_ref[rows, columns] = low


def dot(a, b):
    return jnp.dot(a, b, preferred_element_type=F32)


def multiply(counts, *refs):
    n = len(counts)
    pieces, (high_ref, low_ref, keep_ref, give_ref) = refs[:2 * n], refs[2 * n:]
    slots = sum(counts)
    total = None
    for j in range(2):
        parts = [ref[:count].reshape(64 * count, 2 * B) for count, ref in zip(counts, pieces[j::2])]
        high, low = split(jnp.concatenate(parts, axis=0))
        rows = slice(j * 2 * B, (j + 1) * 2 * B)
        a_high, a_low = high_ref[rows], low_ref[rows]
        term = dot(high, a_high) + (dot(high, a_low) + dot(low, a_high))
        total = term if total is None else total + term
    keep_ref[...] = total[:, :B].reshape(slots, 64, B)
    give_ref[...] = total[:, B:].reshape(slots, 64, B)


def product(pieces, a_high, a_low):
    counts = tuple(piece.shape[0] for piece in pieces[::2])
    slots = sum(counts)
    shape = ((slots, 64, B), F32)
    return call(
        lambda *refs: multiply(counts, *refs),
        [shape, shape],
        *pieces,
        a_high,
        a_low,
        flops=2 * slots * 64 * 2 * B * 4 * B * 3,
    )


def arrange(own_early, own_late, got_early, got_late, *outs):
    child, _, z, core, prow, _ = position()
    x = prow // 2
    early = own_early.shape[0]
    for i, out_ref in enumerate(outs):
        m, flip = i // 2, 1 - i % 2
        target = (x + m) % 4
        w_low = target // 2
        for odd in range(2):
            z_from = 4 * (target % 2) + 2 * (child + flip - 2 * child * flip) + odd
            ahead = (z - z_from + 8) % 8
            near = jnp.logical_or(ahead == 0, ahead == 4)
            source = jnp.where(near, w_low, jnp.where(ahead < 4, 0, 1))
            steps = jnp.where(ahead <= 4, ahead, 8 - ahead)
            inner = 2 * steps - 1 + jnp.where(source == w_low, 0, 1)
            slot = jnp.where(ahead == 0, 0, inner)
            here = source == core
            first = slot < early
            for ref, mine, start in (
                (own_early, True, 0), (own_late, True, early), (got_early, False, 0), (got_late, False, early),
            ):
                wanted = jnp.logical_and(here == mine, first == (start == 0))

                @pl.when(wanted)
                def _():
                    out_ref[odd] = ref[slot - start]


def finish(pattern_ref, own_flip, own_same, got_flip, got_same, out_ref):
    high, _, _, core, _, pcol = position()
    pair = pcol // 2
    for child in range(2):
        here = pattern_ref[child, pair] - 2 * pair == core
        for flip, own, got in ((0, own_same, got_same), (1, own_flip, got_flip)):
            active = (high + child) % 2 == flip

            @pl.when(jnp.logical_and(here, active))
            def _():
                for odd in range(2):
                    mine, theirs = own[odd], got[odd]
                    first = jnp.where(core == 0, mine, theirs)
                    second = jnp.where(core == 0, theirs, mine)
                    block = jnp.concatenate([first, second], axis=0)
                    out_ref[:, child, odd * H:(odd + 1) * H] = -block.T

        @pl.when(jnp.logical_not(here))
        def _():
            out_ref[:, child, :] = jnp.zeros((B, B), F32)


def after(value, *others):
    return lax.optimization_barrier((value, *others))[0]


def per_device(anc_inverse, lpanel, pattern):
    panel = jnp.transpose(lpanel, (1, 2, 0))
    half_piece = ((64, 2 * B), F32)
    mine, other = call(compact_panel, [half_piece, half_piece], pattern, panel)
    columns = [send(mine, spread(0)), send(other, spread(1))]

    pair = ((2, H, 2 * B), F32)
    keep, give = call(compact_inverse, [pair, pair], pattern, anc_inverse)
    got = send(give, other_core)
    quarter = ((H, 2 * B), F32)
    a_mine, a_other = call(choose_rows, [quarter, quarter], pattern, keep, got)
    blocks = [a_mine, send(a_other, other_high), send(a_mine, other_low), send(a_other, other_both)]

    columns = lax.optimization_barrier(columns + [a_mine])[:2]
    pairs = lax.optimization_barrier([jnp.stack([part, send(part, other_core)]) for part in columns])
    early = [pairs[0][:1], pairs[1][:1]]
    for step in range(3):
        if step:
            pairs[0] = after(pairs[0], blocks[step])
        pairs = [send(part, ring) for part in pairs]
        early += pairs
    last = send(jnp.concatenate([part[:1] for part in pairs]), ring)
    late = [last[:1], last[1:]]

    blocks[3] = after(blocks[3], *pairs)
    halves = [send(block, other_core) for block in blocks]
    whole = ((4 * B, 2 * B), BF16)
    a_high, a_low = call(split_inverse, [whole, whole], *blocks, *halves)
    keep_early, give_early = product(early, a_high, a_low)
    keep_late, give_late = product(late, a_high, a_low)
    got_early = send(after(give_early, last), other_core)
    got_late = send(give_late, other_core)
    terms = call(arrange, [((2, 64, B), F32)] * 8, keep_early, keep_late, got_early, got_late)
    moved = list(terms[:2]) + [send(terms[2 * m + i], along_x(m)) for i in range(2) for m in range(1, 4)]
    result = [moved[i] + moved[2 + 3 * i] + moved[3 + 3 * i] + moved[4 + 3 * i] for i in range(2)]
    result = [send(result[0], spread(1)), send(result[1], spread(0))]
    second = [send(part, other_core) for part in result]
    return call(finish, [((B, 2, B), F32)], pattern, *result, *second)[0]


def solution(mesh):
    return jax.shard_map(
        per_device,
        mesh=mesh,
        in_specs=(P("pcol", "prow"), P("prow", None, "pcol"), P()),
        out_specs=P("pcol", None, "prow"),
        check_vma=False,
    )
```

```python
import jax
import jax.numpy as jnp
from jax import lax
from jax.experimental import pallas as pl
from jax.experimental.pallas import tpu as pltpu
from jax.sharding import PartitionSpec as P

B = 256
H = 128
F32 = jnp.float32
BF16 = jnp.bfloat16
AXES = ("prow", "pcol")
VMEM_LIMIT = 40 * 1024 * 1024

DEVICES = [(x, y, z, c) for x in range(4) for y in range(4) for z in range(8) for c in range(2)]


def number(x, y, z, c):
    return (2 * x + y // 2) * 32 + 16 * (y % 2) + 2 * z + c


def send(array, move):
    pairs = [(number(*d), number(*move(*d))) for d in DEVICES]
    return lax.ppermute(array, AXES, pairs)


def other_core(x, y, z, c):
    return x, y, z, 1 - c


def other_low(x, y, z, c):
    return x, y ^ 1, z, c


def other_high(x, y, z, c):
    return x, y ^ 2, z, c


def other_both(x, y, z, c):
    return x, y ^ 3, z, c


def ring(x, y, z, c):
    return x, y, (z + 1 - 2 * c) % 8, c


def along_x(step):
    return lambda x, y, z, c: ((x + step) % 4, y, z, c)


def spread(flip):
    return lambda x, y, z, c: (x, 2 * (y // 2 ^ flip) + c, z, y % 2)


def position():
    prow, pcol = lax.axis_index("prow"), lax.axis_index("pcol")
    return prow % 2, pcol // 16, (pcol // 2) % 8, pcol % 2, prow, pcol


def call(kernel, shapes, *args, flops=0):
    in_specs = [
        pl.BlockSpec(memory_space=pltpu.SMEM if a.dtype == jnp.int32 else pltpu.VMEM) for a in args
    ]
    shapes = [jax.ShapeDtypeStruct(s, d) for s, d in shapes]
    size = sum(a.size * a.dtype.itemsize for a in (*args, *shapes))
    return pl.pallas_call(
        kernel,
        out_shape=shapes,
        in_specs=in_specs,
        out_specs=[pl.BlockSpec(memory_space=pltpu.VMEM) for _ in shapes],
        compiler_params=pltpu.CompilerParams(vmem_limit_bytes=VMEM_LIMIT),
        cost_estimate=pl.CostEstimate(flops=flops, bytes_accessed=size, transcendentals=0),
    )(*args)


def column(pattern_ref, child, prow, t):
    block = pattern_ref[child, 2 * prow + t] - 4 * prow
    return pl.multiple_of(block * B, B)


def compact_panel(pattern_ref, panel_ref, mine_ref, other_ref):
    child, _, _, _, prow, _ = position()
    for out_ref, which in ((mine_ref, child), (other_ref, 1 - child)):
        for t in range(2):
            start = column(pattern_ref, which, prow, t)
            out_ref[:, t * B:(t + 1) * B] = panel_ref[which, :, pl.ds(start, B)]


def compact_inverse(pattern_ref, inverse_ref, keep_ref, give_ref):
    _, _, _, core, prow, _ = position()
    for out_ref, half in ((keep_ref, core), (give_ref, 1 - core)):
        rows = pl.ds(pl.multiple_of(half * H, H), H)
        for child in range(2):
            for t in range(2):
                start = column(pattern_ref, child, prow, t)
                out_ref[child, :, t * B:(t + 1) * B] = inverse_ref[rows, pl.ds(start, B)]


def choose_rows(pattern_ref, own_ref, got_ref, mine_ref, other_ref):
    child, _, _, core, _, pcol = position()
    pair = pcol // 2
    for out_ref, which in ((mine_ref, child), (other_ref, 1 - child)):
        here = pattern_ref[which, pair] - 2 * pair == core

        @pl.when(here)
        def _():
            out_ref[...] = own_ref[which]

        @pl.when(jnp.logical_not(here))
        def _():
            out_ref[...] = got_ref[which]


def split(value):
    high = value.astype(BF16)
    return high, (value - high.astype(F32)).astype(BF16)


def split_inverse(*refs):
    own, got, (high_ref, low_ref) = refs[:4], refs[4:8], refs[8:]
    _, low_y, _, core, _, _ = position()
    for half_refs, half in ((own, core), (got, 1 - core)):
        for i, ref in enumerate(half_refs):
            side = (low_y + core + i // 2) % 2
            high, low = split(ref[...].T)
            rows = slice((i % 2) * 2 * B, (i % 2 + 1) * 2 * B)
            columns = pl.ds(pl.multiple_of(side * B + half * H, H), H)
            high_ref[rows, columns] = high
            low_ref[rows, columns] = low


def dot(a, b):
    return jnp.dot(a, b, preferred_element_type=F32)


def multiply(counts, *refs):
    n = len(counts)
    pieces, (high_ref, low_ref, keep_ref, give_ref) = refs[:2 * n], refs[2 * n:]
    slots = sum(counts)
    total = None
    for j in range(2):
        parts = [ref[:count].reshape(64 * count, 2 * B) for count, ref in zip(counts, pieces[j::2])]
        high, low = split(jnp.concatenate(parts, axis=0))
        rows = slice(j * 2 * B, (j + 1) * 2 * B)
        a_high, a_low = high_ref[rows], low_ref[rows]
        term = dot(high, a_high) + (dot(high, a_low) + dot(low, a_high))
        total = term if total is None else total + term
    keep_ref[...] = total[:, :B].reshape(slots, 64, B)
    give_ref[...] = total[:, B:].reshape(slots, 64, B)


def product(pieces, a_high, a_low):
    counts = tuple(piece.shape[0] for piece in pieces[::2])
    slots = sum(counts)
    shape = ((slots, 64, B), F32)
    return call(
        lambda *refs: multiply(counts, *refs),
        [shape, shape],
        *pieces,
        a_high,
        a_low,
        flops=2 * slots * 64 * 2 * B * 4 * B * 3,
    )


def arrange(own_early, own_late, got_early, got_late, *outs):
    child, _, z, core, prow, _ = position()
    x = prow // 2
    early = own_early.shape[0]
    for i, out_ref in enumerate(outs):
        m, flip = i // 2, 1 - i % 2
        target = (x + m) % 4
        w_low = target // 2
        for odd in range(2):
            z_from = 4 * (target % 2) + 2 * (child + flip - 2 * child * flip) + odd
            ahead = (z - z_from + 8) % 8
            near = jnp.logical_or(ahead == 0, ahead == 4)
            source = jnp.where(near, w_low, jnp.where(ahead < 4, 0, 1))
            steps = jnp.where(ahead <= 4, ahead, 8 - ahead)
            inner = 2 * steps - 1 + jnp.where(source == w_low, 0, 1)
            slot = jnp.where(ahead == 0, 0, inner)
            here = source == core
            first = slot < early
            for ref, mine, start in (
                (own_early, True, 0), (own_late, True, early), (got_early, False, 0), (got_late, False, early),
            ):
                wanted = jnp.logical_and(here == mine, first == (start == 0))

                @pl.when(wanted)
                def _():
                    out_ref[odd] = ref[slot - start]


def finish(pattern_ref, own_flip, own_same, got_flip, got_same, out_ref):
    high, _, _, core, _, pcol = position()
    pair = pcol // 2
    for child in range(2):
        here = pattern_ref[child, pair] - 2 * pair == core
        for flip, own, got in ((0, own_same, got_same), (1, own_flip, got_flip)):
            active = (high + child) % 2 == flip

            @pl.when(jnp.logical_and(here, active))
            def _():
                for odd in range(2):
                    mine, theirs = own[odd], got[odd]
                    first = jnp.where(core == 0, mine, theirs)
                    second = jnp.where(core == 0, theirs, mine)
                    block = jnp.concatenate([first, second], axis=0)
                    out_ref[:, child, odd * H:(odd + 1) * H] = -block.T

        @pl.when(jnp.logical_not(here))
        def _():
            out_ref[:, child, :] = jnp.zeros((B, B), F32)


def after(value, *others):
    return lax.optimization_barrier((value, *others))[0]


def per_device(anc_inverse, lpanel, pattern):
    panel = jnp.transpose(lpanel, (1, 2, 0))
    half_piece = ((64, 2 * B), F32)
    mine, other = call(compact_panel, [half_piece, half_piece], pattern, panel)
    columns = [send(mine, spread(0)), send(other, spread(1))]

    pair = ((2, H, 2 * B), F32)
    keep, give = call(compact_inverse, [pair, pair], pattern, anc_inverse)
    got = send(give, other_core)
    quarter = ((H, 2 * B), F32)
    a_mine, a_other = call(choose_rows, [quarter, quarter], pattern, keep, got)
    blocks = [a_mine, send(a_other, other_high), send(a_mine, other_low), send(a_other, other_both)]

    columns = lax.optimization_barrier(columns + [a_mine])[:2]
    pairs = lax.optimization_barrier([jnp.stack([part, send(part, other_core)]) for part in columns])
    early = [pairs[0][:1], pairs[1][:1]]
    for step in range(3):
        if step:
            pairs[0] = after(pairs[0], blocks[step + 1])
        pairs = [send(part, ring) for part in pairs]
        early += pairs
    last = send(jnp.concatenate([part[:1] for part in pairs]), ring)
    late = [last[:1], last[1:]]

    blocks[1] = after(blocks[1], *pairs)
    halves = [send(block, other_core) for block in blocks]
    whole = ((4 * B, 2 * B), BF16)
    a_high, a_low = call(split_inverse, [whole, whole], *blocks, *halves)
    keep_early, give_early = product(early, a_high, a_low)
    keep_late, give_late = product(late, a_high, a_low)
    got_early = send(after(give_early, last), other_core)
    got_late = send(give_late, other_core)
    terms = call(arrange, [((2, 64, B), F32)] * 8, keep_early, keep_late, got_early, got_late)
    moved = list(terms[:2]) + [send(terms[2 * m + i], along_x(m)) for i in range(2) for m in range(1, 4)]
    result = [moved[i] + moved[2 + 3 * i] + moved[3 + 3 * i] + moved[4 + 3 * i] for i in range(2)]
    result = [send(result[0], spread(1)), send(result[1], spread(0))]
    second = [send(part, other_core) for part in result]
    return call(finish, [((B, 2, B), F32)], pattern, *result, *second)[0]


def solution(mesh):
    return jax.shard_map(
        per_device,
        mesh=mesh,
        in_specs=(P("pcol", "prow"), P("prow", None, "pcol"), P()),
        out_specs=P("pcol", None, "prow"),
        check_vma=False,
    )
```

```python
import jax
import jax.numpy as jnp
from jax import lax
from jax.experimental import pallas as pl
from jax.experimental.pallas import tpu as pltpu
from jax.sharding import PartitionSpec as P

B = 256
H = 128
F32 = jnp.float32
BF16 = jnp.bfloat16
AXES = ("prow", "pcol")
VMEM_LIMIT = 24 * 1024 * 1024

DEVICES = [(x, y, z, c) for x in range(4) for y in range(4) for z in range(8) for c in range(2)]


def number(x, y, z, c):
    return (2 * x + y // 2) * 32 + 16 * (y % 2) + 2 * z + c


def send(array, move):
    pairs = [(number(*d), number(*move(*d))) for d in DEVICES]
    return lax.ppermute(array, AXES, pairs)


def other_core(x, y, z, c):
    return x, y, z, 1 - c


def other_low(x, y, z, c):
    return x, y ^ 1, z, c


def other_high(x, y, z, c):
    return x, y ^ 2, z, c


def other_both(x, y, z, c):
    return x, y ^ 3, z, c


def ring(x, y, z, c):
    return x, y, (z + 1 - 2 * c) % 8, c


def along_x(step):
    return lambda x, y, z, c: ((x + step) % 4, y, z, c)


def spread(flip):
    return lambda x, y, z, c: (x, 2 * (y // 2 ^ flip) + c, z, y % 2)


def position():
    prow, pcol = lax.axis_index("prow"), lax.axis_index("pcol")
    return prow % 2, pcol // 16, (pcol // 2) % 8, pcol % 2, prow, pcol


def call(kernel, shapes, *args, flops=0):
    in_specs = [
        pl.BlockSpec(memory_space=pltpu.SMEM if a.dtype == jnp.int32 else pltpu.VMEM) for a in args
    ]
    shapes = [jax.ShapeDtypeStruct(s, d) for s, d in shapes]
    size = sum(a.size * a.dtype.itemsize for a in (*args, *shapes))
    return pl.pallas_call(
        kernel,
        out_shape=shapes,
        in_specs=in_specs,
        out_specs=[pl.BlockSpec(memory_space=pltpu.VMEM) for _ in shapes],
        compiler_params=pltpu.CompilerParams(vmem_limit_bytes=VMEM_LIMIT),
        cost_estimate=pl.CostEstimate(flops=flops, bytes_accessed=size, transcendentals=0),
    )(*args)


def column(pattern_ref, child, prow, t):
    block = pattern_ref[child, 2 * prow + t] - 4 * prow
    return pl.multiple_of(block * B, B)


def compact_panel(pattern_ref, panel_ref, mine_ref, other_ref):
    child, _, _, _, prow, _ = position()
    for out_ref, which in ((mine_ref, child), (other_ref, 1 - child)):
        for t in range(2):
            start = column(pattern_ref, which, prow, t)
            out_ref[:, t * B:(t + 1) * B] = panel_ref[which, :, pl.ds(start, B)]


def compact_inverse(pattern_ref, inverse_ref, keep_ref, give_ref):
    _, _, _, core, prow, _ = position()
    for out_ref, half in ((keep_ref, core), (give_ref, 1 - core)):
        rows = pl.ds(pl.multiple_of(half * H, H), H)
        for child in range(2):
            for t in range(2):
                start = column(pattern_ref, child, prow, t)
                out_ref[child, :, t * B:(t + 1) * B] = inverse_ref[rows, pl.ds(start, B)]


def choose_rows(pattern_ref, own_ref, got_ref, mine_ref, other_ref):
    child, _, _, core, _, pcol = position()
    pair = pcol // 2
    for out_ref, which in ((mine_ref, child), (other_ref, 1 - child)):
        here = pattern_ref[which, pair] - 2 * pair == core

        @pl.when(here)
        def _():
            out_ref[...] = own_ref[which]

        @pl.when(jnp.logical_not(here))
        def _():
            out_ref[...] = got_ref[which]


def split(value):
    high = value.astype(BF16)
    return high, (value - high.astype(F32)).astype(BF16)


def split_inverse(*refs):
    own, got, (high_ref, low_ref) = refs[:4], refs[4:8], refs[8:]
    _, low_y, _, core, _, _ = position()
    for half_refs, half in ((own, core), (got, 1 - core)):
        for i, ref in enumerate(half_refs):
            side = (low_y + core + i // 2) % 2
            high, low = split(ref[...].T)
            rows = slice((i % 2) * 2 * B, (i % 2 + 1) * 2 * B)
            columns = pl.ds(pl.multiple_of(side * B + half * H, H), H)
            high_ref[rows, columns] = high
            low_ref[rows, columns] = low


def dot(a, b):
    return jnp.dot(a, b, preferred_element_type=F32)


def multiply(counts, *refs):
    n = len(counts)
    pieces, (high_ref, low_ref, keep_ref, give_ref) = refs[:2 * n], refs[2 * n:]
    slots = sum(counts)
    total = None
    for j in range(2):
        parts = [ref[:count].reshape(64 * count, 2 * B) for count, ref in zip(counts, pieces[j::2])]
        high, low = split(jnp.concatenate(parts, axis=0))
        rows = slice(j * 2 * B, (j + 1) * 2 * B)
        a_high, a_low = high_ref[rows], low_ref[rows]
        term = dot(high, a_high) + (dot(high, a_low) + dot(low, a_high))
        total = term if total is None else total + term
    keep_ref[...] = total[:, :B].reshape(slots, 64, B)
    give_ref[...] = total[:, B:].reshape(slots, 64, B)


def product(pieces, a_high, a_low):
    counts = tuple(piece.shape[0] for piece in pieces[::2])
    slots = sum(counts)
    shape = ((slots, 64, B), F32)
    return call(
        lambda *refs: multiply(counts, *refs),
        [shape, shape],
        *pieces,
        a_high,
        a_low,
        flops=2 * slots * 64 * 2 * B * 4 * B * 3,
    )


def arrange(own_early, own_late, got_early, got_late, *outs):
    child, _, z, core, prow, _ = position()
    x = prow // 2
    early = own_early.shape[0]
    for i, out_ref in enumerate(outs):
        m, flip = i // 2, 1 - i % 2
        target = (x + m) % 4
        w_low = target // 2
        for odd in range(2):
            z_from = 4 * (target % 2) + 2 * (child + flip - 2 * child * flip) + odd
            ahead = (z - z_from + 8) % 8
            near = jnp.logical_or(ahead == 0, ahead == 4)
            source = jnp.where(near, w_low, jnp.where(ahead < 4, 0, 1))
            steps = jnp.where(ahead <= 4, ahead, 8 - ahead)
            inner = 2 * steps - 1 + jnp.where(source == w_low, 0, 1)
            slot = jnp.where(ahead == 0, 0, inner)
            here = source == core
            first = slot < early
            for ref, mine, start in (
                (own_early, True, 0), (own_late, True, early), (got_early, False, 0), (got_late, False, early),
            ):
                wanted = jnp.logical_and(here == mine, first == (start == 0))

                @pl.when(wanted)
                def _():
                    out_ref[odd] = ref[slot - start]


def finish(pattern_ref, own_flip, own_same, got_flip, got_same, out_ref):
    high, _, _, core, _, pcol = position()
    pair = pcol // 2
    for child in range(2):
        here = pattern_ref[child, pair] - 2 * pair == core
        for flip, own, got in ((0, own_same, got_same), (1, own_flip, got_flip)):
            active = (high + child) % 2 == flip

            @pl.when(jnp.logical_and(here, active))
            def _():
                for odd in range(2):
                    mine, theirs = own[odd], got[odd]
                    first = jnp.where(core == 0, mine, theirs)
                    second = jnp.where(core == 0, theirs, mine)
                    block = jnp.concatenate([first, second], axis=0)
                    out_ref[:, child, odd * H:(odd + 1) * H] = -block.T

        @pl.when(jnp.logical_not(here))
        def _():
            out_ref[:, child, :] = jnp.zeros((B, B), F32)


def after(value, *others):
    return lax.optimization_barrier((value, *others))[0]


def per_device(anc_inverse, lpanel, pattern):
    panel = jnp.transpose(lpanel, (1, 2, 0))
    half_piece = ((64, 2 * B), F32)
    mine, other = call(compact_panel, [half_piece, half_piece], pattern, panel)
    columns = [send(mine, spread(0)), send(other, spread(1))]

    pair = ((2, H, 2 * B), F32)
    keep, give = call(compact_inverse, [pair, pair], pattern, anc_inverse)
    got = send(give, other_core)
    quarter = ((H, 2 * B), F32)
    a_mine, a_other = call(choose_rows, [quarter, quarter], pattern, keep, got)
    blocks = [a_mine, send(a_other, other_high), send(a_mine, other_low), send(a_other, other_both)]

    columns = lax.optimization_barrier(columns + [a_mine])[:2]
    pairs = lax.optimization_barrier([jnp.stack([part, send(part, other_core)]) for part in columns])
    early = [pairs[0][:1], pairs[1][:1]]
    for step in range(3):
        if step:
            pairs[0] = after(pairs[0], blocks[step + 1])
        pairs = [send(part, ring) for part in pairs]
        early += pairs
    last = send(jnp.concatenate([part[:1] for part in pairs]), ring)
    late = [last[:1], last[1:]]

    blocks[1] = after(blocks[1], *pairs)
    halves = [send(block, other_core) for block in blocks]
    whole = ((4 * B, 2 * B), BF16)
    a_high, a_low = call(split_inverse, [whole, whole], *blocks, *halves)
    keep_early, give_early = product(early, a_high, a_low)
    keep_late, give_late = product(late, a_high, a_low)
    got_early = send(give_early, other_core)
    got_late = send(give_late, other_core)
    terms = call(arrange, [((2, 64, B), F32)] * 8, keep_early, keep_late, got_early, got_late)
    moved = list(terms[:2]) + [send(terms[2 * m + i], along_x(m)) for i in range(2) for m in range(1, 4)]
    result = [moved[i] + moved[2 + 3 * i] + moved[3 + 3 * i] + moved[4 + 3 * i] for i in range(2)]
    result = [send(result[0], spread(1)), send(result[1], spread(0))]
    second = [send(part, other_core) for part in result]
    return call(finish, [((B, 2, B), F32)], pattern, *result, *second)[0]


def solution(mesh):
    return jax.shard_map(
        per_device,
        mesh=mesh,
        in_specs=(P("pcol", "prow"), P("prow", None, "pcol"), P()),
        out_specs=P("pcol", None, "prow"),
        check_vma=False,
    )
```
